32 devices in a mesh: dp: 8 (over z, y), cent: 4 (over x, core).
Axes of the slice: x: 2, y: 2, z: 4, core: 2. Of those that a mesh axis runs over, the one named last changes fastest.
Arguments:
- embeddings: bfloat16 [6144, 768], P('dp'), may hold values from -40 to 40
- centroids: bfloat16 [16384, 768], P('cent'), may hold values from -5 to 5
- rotation: float32 [768, 768], replicated, may hold values from -1 to 2
Outputs:
- new_centroids: float32 [16384, 768], P(('cent', 'dp'))
- new_rotation: float32 [768, 768], replicated
The draws below stay inside these ranges and needn't reach their ends.
All inputs are finite; a program needn't handle non-finite values.
Results may differ from the reference program's by a relative error of at most 0.0042.
Values sent between devices are 32-bit elements; how exact they have to be, the bound alone decides.
A program may use at most 128 MiB of HBM per device.

```python
import math
import jax
import jax.numpy as jnp
from jax import lax

D = 768
ROWS_DEV = 768
NS_ITERS = 4
CENTROIDS = 16384
ROWS = 6144


def base_rows(key):
    return jnp.clip(jax.random.normal(jax.random.fold_in(key, 99), (CENTROIDS, D), jnp.float32), -5.0, 5.0)


def draw_embeddings(key, part):
    values = jnp.clip(jax.random.normal(jax.random.fold_in(key, 1), (ROWS, D), jnp.float32), -6.0, 6.0)
    return values.astype(jnp.bfloat16)


def draw_centroids(key, part):
    values = base_rows(key)
    return values.astype(jnp.bfloat16)


def draw_rotation(key, part):
    noise = jnp.clip(jax.random.normal(jax.random.fold_in(key, 4), (D, D), jnp.float32), -4.0, 4.0)
    return (jnp.eye(D, dtype=jnp.float32) + 0.5 / math.sqrt(D) * noise).astype(jnp.float32)


def setup_inputs(seed: int = 0) -> dict:
    splits = jax.random.split(jax.random.key(seed), 4)
    return {
        "embeddings": draw_embeddings(jax.random.fold_in(splits[3], 71), 0),
        "centroids": draw_centroids(jax.random.fold_in(splits[3], 71), 0),
        "rotation": draw_rotation(jax.random.fold_in(splits[3], 71), 0),
    }


SHARPNESS = 3.0
PRIOR_WEIGHT = 0.25
EPSILON = 1e-06

def polar_update(cross_gram):
    highest = lax.Precision.HIGHEST
    frobenius = jnp.sqrt(jnp.sum(cross_gram * cross_gram) + EPSILON)
    unit_cross = cross_gram / frobenius
    gram_once = jnp.dot(unit_cross.T, unit_cross, precision=highest)
    gram_twice = jnp.dot(gram_once, gram_once, precision=highest)
    norm_scale = (jnp.sum(gram_twice * gram_twice) + EPSILON) ** 0.125
    iterate = unit_cross / norm_scale
    for iteration in range(NS_ITERS):
        inner = jnp.dot(iterate.T, iterate, precision=highest)
        iterate = 1.5 * iterate - 0.5 * jnp.dot(iterate, inner, precision=highest)
    return iterate

def reference(embeddings, centroids, rotation):
    highest = lax.Precision.HIGHEST
    half_norm = 0.5 * lax.optimization_barrier(jnp.sum(jnp.square(centroids.astype(jnp.float32)), axis=1))
    score_scale = SHARPNESS / math.sqrt(D)
    block_count = ROWS // ROWS_DEV
    emb_blocks = embeddings.reshape(block_count, ROWS_DEV, D)

    def one_block(carry, row_block):
        cent_sums, counts, cross_gram = carry
        rows_wide = row_block.astype(jnp.float32)
        rotated = jnp.dot(rows_wide, rotation, precision=highest).astype(jnp.bfloat16)
        scores = (jnp.dot(rotated, centroids.T, preferred_element_type=jnp.float32) - half_norm[None, :]) * score_scale
        row_top = lax.optimization_barrier(jnp.max(scores, axis=1))
        exp_scores = jnp.exp(scores - row_top[:, None])
        row_total = lax.optimization_barrier(jnp.sum(exp_scores, axis=1))
        weights = (exp_scores / row_total[:, None]).astype(jnp.bfloat16)
        cent_sums = cent_sums + jnp.dot(weights.T, rotated, preferred_element_type=jnp.float32)
        counts = counts + lax.optimization_barrier(jnp.sum(weights.astype(jnp.float32), axis=0))
        rebuilt = jnp.dot(weights, centroids, preferred_element_type=jnp.float32)
        cross_gram = cross_gram + jnp.dot(rows_wide.T, rebuilt, precision=highest)
        return ((cent_sums, counts, cross_gram), None)
    start_state = (jnp.zeros((CENTROIDS, D), jnp.float32), jnp.zeros((CENTROIDS,), jnp.float32), jnp.zeros((D, D), jnp.float32))
    (cent_sums, counts, cross_gram), unused = lax.scan(one_block, start_state, emb_blocks)
    new_centroids = (cent_sums + PRIOR_WEIGHT * centroids.astype(jnp.float32)) / (counts + PRIOR_WEIGHT)[:, None]
    return (new_centroids, polar_update(cross_gram))
```

```python
import functools
import math

import jax
import jax.numpy as jnp
from jax import lax
from jax.experimental import pallas as pl
from jax.experimental.pallas import tpu as pltpu
from jax.sharding import PartitionSpec as P

NS_ITERS = 4
SHARPNESS = 3.0
PRIOR_WEIGHT = 0.25
EPSILON = 1e-06
GROUP = 4
TILE = 512
VMEM_BYTES = 56 * 1024 * 1024

f32, bf16 = jnp.float32, jnp.bfloat16


def dot(a, b, ca, cb):
    return lax.dot_general(a, b, (((ca,), (cb,)), ((), ())), preferred_element_type=f32)


def half_norms(block):
    wide = block.astype(f32)
    return 0.5 * jnp.sum(wide * wide, axis=1, keepdims=True)


def stats_kernel(scale, rot_ref, cent_ref, exp_ref, tile_top_ref, stat_ref, rot_s, run_s):
    step = pl.program_id(0)

    @pl.when(step == 0)
    def _():
        rot_s[...] = rot_ref[...].astype(bf16)
        run_s[0:1, :] = jnp.full((1, run_s.shape[1]), -jnp.inf, f32)
        run_s[1:2, :] = jnp.zeros((1, run_s.shape[1]), f32)

    cents = cent_ref[...]
    scores = (dot(cents, rot_s[...], 1, 1) - half_norms(cents)) * scale
    old_top = run_s[0:1, :]
    top = jnp.maximum(old_top, jnp.max(scores, axis=0, keepdims=True))
    exps = jnp.exp(scores - top)
    total = run_s[1:2, :] * jnp.exp(old_top - top) + jnp.sum(exps, axis=0, keepdims=True)
    exp_ref[...] = exps
    tile_top_ref[0] = top
    run_s[0:1, :] = top
    run_s[1:2, :] = total
    stat_ref[0:1, :] = top
    stat_ref[1:2, :] = total


def row_stats(rot, centroids, scale):
    rows, width = rot.shape
    count = centroids.shape[0]
    tiles = count // TILE
    return pl.pallas_call(
        functools.partial(stats_kernel, scale),
        grid=(tiles,),
        in_specs=[
            pl.BlockSpec((rows, width), lambda i: (0, 0)),
            pl.BlockSpec((TILE, width), lambda i: (i, 0)),
        ],
        out_specs=[
            pl.BlockSpec((TILE, rows), lambda i: (i, 0)),
            pl.BlockSpec((1, 1, rows), lambda i: (i, 0, 0)),
            pl.BlockSpec((2, rows), lambda i: (0, 0)),
        ],
        out_shape=[
            jax.ShapeDtypeStruct((count, rows), f32),
            jax.ShapeDtypeStruct((tiles, 1, rows), f32),
            jax.ShapeDtypeStruct((2, rows), f32),
        ],
        scratch_shapes=[pltpu.VMEM((rows, width), bf16), pltpu.VMEM((8, rows), f32)],
        compiler_params=pltpu.CompilerParams(vmem_limit_bytes=VMEM_BYTES),
        cost_estimate=pl.CostEstimate(
            flops=2 * rows * width * count, bytes_accessed=count * (4 * rows + 2 * width), transcendentals=rows * count
        ),
        name="row_stats",
    )(rot, centroids)


def cross_kernel(tiles, exp_ref, tile_top_ref, stat_ref, cent_ref, emb_ref, cross_ref, acc):
    step = pl.program_id(0)
    factor = jnp.exp(tile_top_ref[0] - stat_ref[0:1, :]) * stat_ref[1:2, :]
    weights = (exp_ref[...] * factor).astype(bf16)
    part = dot(weights, cent_ref[...], 0, 0)

    @pl.when(step == 0)
    def _():
        acc[...] = part

    @pl.when(step > 0)
    def _():
        acc[...] += part

    @pl.when(step == tiles - 1)
    def _():
        rebuilt = acc[...]
        high = rebuilt.astype(bf16)
        low = (rebuilt - high.astype(f32)).astype(bf16)
        emb = emb_ref[...]
        cross_ref[...] = dot(emb, high, 0, 0) + dot(emb, low, 0, 0)


def cross_partial(exps, tile_tops, stats, centroids, embeddings):
    count, rows = exps.shape
    width = centroids.shape[1]
    tiles = count // TILE
    return pl.pallas_call(
        functools.partial(cross_kernel, tiles),
        grid=(tiles,),
        in_specs=[
            pl.BlockSpec((TILE, rows), lambda i: (i, 0)),
            pl.BlockSpec((1, 1, rows), lambda i: (i, 0, 0)),
            pl.BlockSpec((2, rows), lambda i: (0, 0)),
            pl.BlockSpec((TILE, width), lambda i: (i, 0)),
            pl.BlockSpec((rows, width), lambda i: (0, 0)),
        ],
        out_specs=pl.BlockSpec((width, width), lambda i: (0, 0)),
        out_shape=jax.ShapeDtypeStruct((width, width), f32),
        scratch_shapes=[pltpu.VMEM((rows, width), f32)],
        compiler_params=pltpu.CompilerParams(vmem_limit_bytes=VMEM_BYTES),
        cost_estimate=pl.CostEstimate(
            flops=2 * rows * width * count, bytes_accessed=count * (4 * rows + 2 * width), transcendentals=0
        ),
        name="cross_partial",
    )(exps, tile_tops, stats, centroids, embeddings)


def sums_kernel(scale, rows_ref, stat_ref, cent_ref, sums_ref, counts_ref, rows_s):
    @pl.when(pl.program_id(0) == 0)
    def _():
        rows_s[...] = rows_ref[...].astype(bf16)

    cents = cent_ref[0].astype(bf16)
    rot = rows_s[...]
    scores = (dot(cents, rot, 1, 1) - half_norms(cents)) * scale
    weights = (jnp.exp(scores - stat_ref[0:1, :]) * stat_ref[1:2, :]).astype(bf16)
    sums_ref[0] = dot(weights, rot, 1, 0)
    counts = jnp.sum(weights.astype(f32), axis=1, keepdims=True)
    counts_ref[0] = jnp.broadcast_to(counts, counts_ref.shape[1:])


def cent_partial(rows, stats, blocks, scale):
    count, width = rows.shape
    number, block, _ = blocks.shape
    return pl.pallas_call(
        functools.partial(sums_kernel, scale),
        grid=(number,),
        in_specs=[
            pl.BlockSpec((count, width), lambda i: (0, 0)),
            pl.BlockSpec((2, count), lambda i: (0, 0)),
            pl.BlockSpec((1, block, width), lambda i: (i, 0, 0)),
        ],
        out_specs=[
            pl.BlockSpec((1, block, width), lambda i: (i, 0, 0)),
            pl.BlockSpec((1, block, 128), lambda i: (i, 0, 0)),
        ],
        out_shape=[
            jax.ShapeDtypeStruct((number, block, width), f32),
            jax.ShapeDtypeStruct((number, block, 128), f32),
        ],
        scratch_shapes=[pltpu.VMEM((count, width), bf16)],
        compiler_params=pltpu.CompilerParams(vmem_limit_bytes=VMEM_BYTES),
        cost_estimate=pl.CostEstimate(
            flops=4 * count * width * number * block,
            bytes_accessed=8 * number * block * width + 4 * count * width,
            transcendentals=count * number * block,
        ),
        name="cent_partial",
    )(rows, stats, blocks)


def split(value):
    high = value.astype(bf16)
    return high, (value - high.astype(f32)).astype(bf16)


def dot3(a, b, ca, cb):
    return dot(a[0], b[0], ca, cb) + dot(a[0], b[1], ca, cb) + dot(a[1], b[0], ca, cb)


def polar_kernel(cross_ref, out_ref, high_s, low_s, gram_s):
    cross = cross_ref[...]
    unit = cross * lax.rsqrt(jnp.sum(cross * cross, keepdims=True) + EPSILON)
    high, low = split(unit)
    high_s[...] = high
    low_s[...] = low
    gram_once = dot3((high, low), (high, low), 0, 0)
    gram_s[...] = gram_once
    pair = split(gram_once)
    gram_twice = dot3(pair, pair, 1, 0)
    norm_power = jnp.sum(gram_twice * gram_twice, keepdims=True) + EPSILON
    inverse = 1.0 / jnp.sqrt(jnp.sqrt(jnp.sqrt(norm_power)))
    pair = split(gram_s[...] * (inverse * inverse))
    product = dot3((high_s[...], low_s[...]), pair, 1, 0)
    out_ref[...] = (1.5 * unit - 0.5 * product) * inverse

    @pl.loop(1, NS_ITERS)
    def _(_):
        pair = split(out_ref[...])
        inner = split(dot3(pair, pair, 0, 0))
        out_ref[...] = 1.5 * out_ref[...] - 0.5 * dot3(pair, inner, 1, 0)


def polar_update(cross):
    width = cross.shape[0]
    return pl.pallas_call(
        polar_kernel,
        in_specs=[pl.BlockSpec(memory_space=pltpu.VMEM)],
        out_specs=pl.BlockSpec(memory_space=pltpu.VMEM),
        out_shape=jax.ShapeDtypeStruct((width, width), f32),
        scratch_shapes=[
            pltpu.VMEM((width, width), bf16),
            pltpu.VMEM((width, width), bf16),
            pltpu.VMEM((width, width), f32),
        ],
        compiler_params=pltpu.CompilerParams(vmem_limit_bytes=VMEM_BYTES),
        cost_estimate=pl.CostEstimate(flops=54 * width**3, bytes_accessed=8 * width**2, transcendentals=0),
        name="polar_update",
    )(cross)


def solution(mesh):
    dp, cent = mesh.shape["dp"], mesh.shape["cent"]
    across_core = [(i, i ^ 1) for i in range(cent)]
    across_x = [(i, i ^ 2) for i in range(cent)]

    def gather_small(value, axis, size):
        slots = jnp.zeros((size, *value.shape), f32)
        slots = lax.dynamic_update_slice_in_dim(slots, value[None], lax.axis_index(axis), 0)
        return lax.psum(slots, axis)

    def body(embeddings, centroids, rotation):
        rows, width = embeddings.shape
        scale = SHARPNESS / math.sqrt(width)
        share = rows // GROUP
        block = centroids.shape[0] // dp
        dp_index = lax.axis_index("dp")
        cent_index = lax.axis_index("cent")
        first_row = lax.rem(cent_index, GROUP) * share

        rotated = jnp.dot(embeddings.astype(f32), rotation, precision=lax.Precision.HIGHEST)
        rotated = lax.reduce_precision(rotated, 8, 7)

        own_rows = lax.dynamic_slice_in_dim(rotated, first_row, share, 0)
        all_rows = lax.all_gather(own_rows, "dp", axis=0, tiled=True)

        own_block = lax.dynamic_slice_in_dim(centroids, dp_index * block, block, 0)
        own_block = lax.optimization_barrier(own_block.astype(f32))
        x_block = lax.ppermute(own_block, "cent", across_x)
        pair = jnp.stack([own_block, x_block])
        other_pair = lax.ppermute(pair, "cent", across_core)
        blocks = jnp.concatenate([pair, other_pair])

        exps, tile_tops, local = row_stats(rotated, centroids, scale)
        gathered = gather_small(local, "cent", cent)
        top = jnp.max(gathered[:, 0], axis=0)
        total = jnp.sum(gathered[:, 1] * jnp.exp(gathered[:, 0] - top), axis=0)
        stats = jnp.stack([top, 1.0 / total])

        cross = lax.psum(cross_partial(exps, tile_tops, stats, centroids, embeddings), ("dp", "cent"))
        new_rotation = polar_update(cross)

        own_stats = lax.dynamic_slice_in_dim(stats, first_row, share, 1)
        all_stats = gather_small(own_stats, "dp", dp)
        all_stats = jnp.swapaxes(all_stats, 0, 1).reshape(2, dp * share)
        sums, counts = cent_partial(all_rows, all_stats, blocks, scale)
        sums = sums[:2] + lax.ppermute(sums[2:], "cent", across_core)
        counts = counts[..., 0]
        counts = counts[:2] + lax.ppermute(counts[2:], "cent", across_core)
        sums = sums[0] + lax.ppermute(sums[1], "cent", across_x)
        counts = counts[0] + lax.ppermute(counts[1], "cent", across_x)
        new_centroids = (sums + PRIOR_WEIGHT * own_block) / (counts + PRIOR_WEIGHT)[:, None]
        return new_centroids, new_rotation

    in_specs = (P("dp", None), P("cent", None), P())
    out_specs = (P(("cent", "dp"), None), P())
    return jax.shard_map(body, mesh=mesh, in_specs=in_specs, out_specs=out_specs, check_vma=False)
```

```python
import functools
import math

import jax
import jax.numpy as jnp
from jax import lax
from jax.experimental import pallas as pl
from jax.experimental.pallas import tpu as pltpu
from jax.sharding import PartitionSpec as P

NS_ITERS = 4
SHARPNESS = 3.0
PRIOR_WEIGHT = 0.25
EPSILON = 1e-06
GROUP = 4
TILE = 512
VMEM_BYTES = 56 * 1024 * 1024

f32, bf16 = jnp.float32, jnp.bfloat16


def dot(a, b, ca, cb):
    return lax.dot_general(a, b, (((ca,), (cb,)), ((), ())), preferred_element_type=f32)


def half_norms(block):
    wide = block.astype(f32)
    return 0.5 * jnp.sum(wide * wide, axis=1, keepdims=True)


def stats_kernel(scale, rot_ref, cent_ref, exp_ref, tile_top_ref, stat_ref, rot_s, run_s):
    step = pl.program_id(0)

    @pl.when(step == 0)
    def _():
        rot_s[...] = rot_ref[...].astype(bf16)
        run_s[0:1, :] = jnp.full((1, run_s.shape[1]), -jnp.inf, f32)
        run_s[1:2, :] = jnp.zeros((1, run_s.shape[1]), f32)

    cents = cent_ref[...]
    scores = (dot(cents, rot_s[...], 1, 1) - half_norms(cents)) * scale
    old_top = run_s[0:1, :]
    top = jnp.maximum(old_top, jnp.max(scores, axis=0, keepdims=True))
    exps = jnp.exp(scores - top)
    total = run_s[1:2, :] * jnp.exp(old_top - top) + jnp.sum(exps, axis=0, keepdims=True)
    exp_ref[...] = exps
    tile_top_ref[0] = top
    run_s[0:1, :] = top
    run_s[1:2, :] = total
    stat_ref[0:1, :] = top
    stat_ref[1:2, :] = total


def row_stats(rot, centroids, scale):
    rows, width = rot.shape
    count = centroids.shape[0]
    tiles = count // TILE
    return pl.pallas_call(
        functools.partial(stats_kernel, scale),
        grid=(tiles,),
        in_specs=[
            pl.BlockSpec((rows, width), lambda i: (0, 0)),
            pl.BlockSpec((TILE, width), lambda i: (i, 0)),
        ],
        out_specs=[
            pl.BlockSpec((TILE, rows), lambda i: (i, 0)),
            pl.BlockSpec((1, 1, rows), lambda i: (i, 0, 0)),
            pl.BlockSpec((2, rows), lambda i: (0, 0)),
        ],
        out_shape=[
            jax.ShapeDtypeStruct((count, rows), f32),
            jax.ShapeDtypeStruct((tiles, 1, rows), f32),
            jax.ShapeDtypeStruct((2, rows), f32),
        ],
        scratch_shapes=[pltpu.VMEM((rows, width), bf16), pltpu.VMEM((8, rows), f32)],
        compiler_params=pltpu.CompilerParams(vmem_limit_bytes=VMEM_BYTES),
        cost_estimate=pl.CostEstimate(
            flops=2 * rows * width * count, bytes_accessed=count * (4 * rows + 2 * width), transcendentals=rows * count
        ),
        name="row_stats",
    )(rot, centroids)


def cross_kernel(tiles, exp_ref, tile_top_ref, stat_ref, cent_ref, emb_ref, cross_ref, acc):
    step = pl.program_id(0)
    factor = jnp.exp(tile_top_ref[0] - stat_ref[0:1, :]) * stat_ref[1:2, :]
    weights = (exp_ref[...] * factor).astype(bf16)
    part = dot(weights, cent_ref[...], 0, 0)

    @pl.when(step == 0)
    def _():
        acc[...] = part

    @pl.when(step > 0)
    def _():
        acc[...] += part

    @pl.when(step == tiles - 1)
    def _():
        rebuilt = acc[...]
        high = rebuilt.astype(bf16)
        low = (rebuilt - high.astype(f32)).astype(bf16)
        emb = emb_ref[...]
        cross_ref[...] = dot(emb, high, 0, 0) + dot(emb, low, 0, 0)


def cross_partial(exps, tile_tops, stats, centroids, embeddings):
    count, rows = exps.shape
    width = centroids.shape[1]
    tiles = count // TILE
    return pl.pallas_call(
        functools.partial(cross_kernel, tiles),
        grid=(tiles,),
        in_specs=[
            pl.BlockSpec((TILE, rows), lambda i: (i, 0)),
            pl.BlockSpec((1, 1, rows), lambda i: (i, 0, 0)),
            pl.BlockSpec((2, rows), lambda i: (0, 0)),
            pl.BlockSpec((TILE, width), lambda i: (i, 0)),
            pl.BlockSpec((rows, width), lambda i: (0, 0)),
        ],
        out_specs=pl.BlockSpec((width, width), lambda i: (0, 0)),
        out_shape=jax.ShapeDtypeStruct((width, width), f32),
        scratch_shapes=[pltpu.VMEM((rows, width), f32)],
        compiler_params=pltpu.CompilerParams(vmem_limit_bytes=VMEM_BYTES),
        cost_estimate=pl.CostEstimate(
            flops=2 * rows * width * count, bytes_accessed=count * (4 * rows + 2 * width), transcendentals=0
        ),
        name="cross_partial",
    )(exps, tile_tops, stats, centroids, embeddings)


def sums_kernel(scale, rows_ref, stat_ref, cent_ref, sums_ref, counts_ref, rows_s):
    @pl.when(pl.program_id(0) == 0)
    def _():
        rows_s[...] = rows_ref[...].astype(bf16)

    cents = cent_ref[0].astype(bf16)
    rot = rows_s[...]
    scores = (dot(cents, rot, 1, 1) - half_norms(cents)) * scale
    weights = (jnp.exp(scores - stat_ref[0:1, :]) * stat_ref[1:2, :]).astype(bf16)
    sums_ref[0] = dot(weights, rot, 1, 0)
    counts = jnp.sum(weights.astype(f32), axis=1, keepdims=True)
    counts_ref[0] = jnp.broadcast_to(counts, counts_ref.shape[1:])


def cent_partial(rows, stats, blocks, scale):
    count, width = rows.shape
    number, block, _ = blocks.shape
    return pl.pallas_call(
        functools.partial(sums_kernel, scale),
        grid=(number,),
        in_specs=[
            pl.BlockSpec((count, width), lambda i: (0, 0)),
            pl.BlockSpec((2, count), lambda i: (0, 0)),
            pl.BlockSpec((1, block, width), lambda i: (i, 0, 0)),
        ],
        out_specs=[
            pl.BlockSpec((1, block, width), lambda i: (i, 0, 0)),
            pl.BlockSpec((1, block, 128), lambda i: (i, 0, 0)),
        ],
        out_shape=[
            jax.ShapeDtypeStruct((number, block, width), f32),
            jax.ShapeDtypeStruct((number, block, 128), f32),
        ],
        scratch_shapes=[pltpu.VMEM((count, width), bf16)],
        compiler_params=pltpu.CompilerParams(vmem_limit_bytes=VMEM_BYTES),
        cost_estimate=pl.CostEstimate(
            flops=4 * count * width * number * block,
            bytes_accessed=8 * number * block * width + 4 * count * width,
            transcendentals=count * number * block,
        ),
        name="cent_partial",
    )(rows, stats, blocks)


def polar_kernel(cross_ref, out_ref, half_s):
    cross = cross_ref[...]
    unit = cross * lax.rsqrt(jnp.sum(cross * cross, keepdims=True) + EPSILON)
    half = unit.astype(bf16)
    half_s[...] = half
    gram_once = dot(half, half, 0, 0)
    gram_half = gram_once.astype(bf16)
    gram_twice = dot(gram_half, gram_half, 1, 0)
    norm_power = jnp.sum(gram_twice * gram_twice, keepdims=True) + EPSILON
    inverse = 1.0 / jnp.sqrt(jnp.sqrt(jnp.sqrt(norm_power)))
    product = dot(half_s[...], gram_half, 1, 0) * (inverse * inverse)
    out_ref[...] = (1.5 * unit - 0.5 * product) * inverse

    @pl.loop(1, NS_ITERS)
    def _(_):
        half_s[...] = out_ref[...].astype(bf16)
        inner = dot(half_s[...], half_s[...], 0, 0).astype(bf16)
        out_ref[...] = 1.5 * out_ref[...] - 0.5 * dot(half_s[...], inner, 1, 0)


def polar_update(cross):
    width = cross.shape[0]
    return pl.pallas_call(
        polar_kernel,
        in_specs=[pl.BlockSpec(memory_space=pltpu.VMEM)],
        out_specs=pl.BlockSpec(memory_space=pltpu.VMEM),
        out_shape=jax.ShapeDtypeStruct((width, width), f32),
        scratch_shapes=[
            pltpu.VMEM((width, width), bf16),
        ],
        compiler_params=pltpu.CompilerParams(vmem_limit_bytes=VMEM_BYTES),
        cost_estimate=pl.CostEstimate(flops=18 * width**3, bytes_accessed=8 * width**2, transcendentals=0),
        name="polar_update",
    )(cross)


def solution(mesh):
    dp, cent = mesh.shape["dp"], mesh.shape["cent"]
    sizes = {"dp": dp, "cent": cent}
    cent_bits = [1 << k for k in range(cent.bit_length() - 1)]
    dp_bits = [1 << k for k in range(dp.bit_length() - 1)]

    def swap(value, axis, bit):
        return lax.ppermute(value, axis, [(i, i ^ bit) for i in range(sizes[axis])])

    def is_upper(axis, bit):
        return lax.rem(lax.div(lax.axis_index(axis), bit), 2)

    def halve(value, axis, bit):
        side, half = is_upper(axis, bit), value.shape[0] // 2
        sent = lax.dynamic_slice_in_dim(value, (1 - side) * half, half, 0)
        kept = lax.dynamic_slice_in_dim(value, side * half, half, 0)
        return kept + swap(sent, axis, bit)

    def double(value, axis, bit):
        other = swap(value, axis, bit)
        upper = is_upper(axis, bit) == 1
        return jnp.concatenate([jnp.where(upper, other, value), jnp.where(upper, value, other)])

    def after(value, earlier):
        return lax.optimization_barrier((value, earlier))[0]

    def sum_part(value, halved, added, earlier):
        for axis, bit in halved:
            value = halve(value, axis, bit)
        for axis, bit in added:
            value = value + swap(value, axis, bit)
        value = after(value, earlier)
        for axis, bit in reversed(halved):
            value = double(value, axis, bit)
        return value

    def sum_everywhere(value, earlier):
        value = halve(value, "cent", 1)
        rows = value.shape[0] // 2
        rest = [("dp", bit) for bit in dp_bits[1:]] + [("cent", bit) for bit in cent_bits[2:]]
        first = sum_part(value[:rows], [("cent", 2), ("dp", 1)], rest, earlier)
        second = sum_part(value[rows:], [("dp", 1), ("cent", 2)], rest, earlier)
        return double(jnp.concatenate([first, second]), "cent", 1)

    def body(embeddings, centroids, rotation):
        rows, width = embeddings.shape
        scale = SHARPNESS / math.sqrt(width)
        share = rows // GROUP
        block = centroids.shape[0] // dp
        dp_index = lax.axis_index("dp")
        cent_index = lax.axis_index("cent")
        first_row = lax.rem(cent_index, GROUP) * share

        rotated = jnp.dot(embeddings.astype(f32), rotation, precision=lax.Precision.HIGHEST)
        rotated = lax.reduce_precision(rotated, 8, 7)

        own_rows = lax.dynamic_slice_in_dim(rotated, first_row, share, 0)
        own_rows = lax.optimization_barrier(own_rows)
        all_rows = lax.all_gather(own_rows, "dp", axis=0, tiled=True)

        own_block = lax.dynamic_slice_in_dim(centroids, dp_index * block, block, 0)
        own_block = lax.optimization_barrier(own_block.astype(f32))
        x_block = swap(own_block, "cent", 2)

        exps, tile_tops, local = row_stats(after(rotated, own_rows), centroids, scale)
        top, total = local[:1], local[1:]
        for bit in cent_bits:
            other = swap(jnp.concatenate([top, total]), "cent", bit)
            new_top = jnp.maximum(top, other[:1])
            total = total * jnp.exp(top - new_top) + other[1:] * jnp.exp(other[:1] - new_top)
            top = new_top
        stats = jnp.concatenate([top, 1.0 / total])

        partial = cross_partial(exps, tile_tops, stats, centroids, embeddings)
        cross = sum_everywhere(partial, all_rows)

        pair = jnp.stack([own_block, after(x_block, partial)])
        other_pair = swap(pair, "cent", 1)
        blocks = jnp.concatenate([pair, other_pair])
        all_stats = after(lax.dynamic_slice_in_dim(stats, first_row, share, 1), partial)[None]
        for bit in dp_bits:
            all_stats = double(all_stats, "dp", bit)
        all_stats = jnp.swapaxes(all_stats, 0, 1).reshape(2, dp * share)
        sums, counts = cent_partial(all_rows, after(all_stats, cross), blocks, scale)
        new_rotation = polar_update(after(cross, counts))
        sums = sums[:2] + swap(sums[2:], "cent", 1)
        counts = counts[..., 0]
        counts = counts[:2] + swap(counts[2:], "cent", 1)
        sums = sums[0] + swap(sums[1], "cent", 2)
        counts = counts[0] + swap(counts[1], "cent", 2)
        new_centroids = (sums + PRIOR_WEIGHT * own_block) / (counts + PRIOR_WEIGHT)[:, None]
        return new_centroids, new_rotation

    in_specs = (P("dp", None), P("cent", None), P())
    out_specs = (P(("cent", "dp"), None), P())
    return jax.shard_map(body, mesh=mesh, in_specs=in_specs, out_specs=out_specs, check_vma=False)
```

```python
import functools
import math

import jax
import jax.numpy as jnp
from jax import lax
from jax.experimental import pallas as pl
from jax.experimental.pallas import tpu as pltpu
from jax.sharding import PartitionSpec as P

NS_ITERS = 4
SHARPNESS = 3.0
PRIOR_WEIGHT = 0.25
EPSILON = 1e-06
GROUP = 4
TILE = 1024
VMEM_BYTES = 56 * 1024 * 1024

f32, bf16 = jnp.float32, jnp.bfloat16


def dot(a, b, ca, cb):
    return lax.dot_general(a, b, (((ca,), (cb,)), ((), ())), preferred_element_type=f32)


def half_norms(block):
    wide = block.astype(f32)
    return 0.5 * jnp.sum(wide * wide, axis=1, keepdims=True)


def stats_kernel(scale, rot_ref, cent_ref, exp_ref, tile_top_ref, stat_ref, rot_s, run_s):
    step = pl.program_id(0)

    @pl.when(step == 0)
    def _():
        rot_s[...] = rot_ref[...].astype(bf16)
        run_s[0:1, :] = jnp.full((1, run_s.shape[1]), -jnp.inf, f32)
        run_s[1:2, :] = jnp.zeros((1, run_s.shape[1]), f32)

    cents = cent_ref[...]
    scores = (dot(cents, rot_s[...], 1, 1) - half_norms(cents)) * scale
    old_top = run_s[0:1, :]
    top = jnp.maximum(old_top, jnp.max(scores, axis=0, keepdims=True))
    exps = jnp.exp(scores - top)
    total = run_s[1:2, :] * jnp.exp(old_top - top) + jnp.sum(exps, axis=0, keepdims=True)
    exp_ref[...] = exps
    tile_top_ref[0] = top
    run_s[0:1, :] = top
    run_s[1:2, :] = total
    stat_ref[0:1, :] = top
    stat_ref[1:2, :] = total


def row_stats(rot, centroids, scale):
    rows, width = rot.shape
    count = centroids.shape[0]
    tiles = count // TILE
    return pl.pallas_call(
        functools.partial(stats_kernel, scale),
        grid=(tiles,),
        in_specs=[
            pl.BlockSpec((rows, width), lambda i: (0, 0)),
            pl.BlockSpec((TILE, width), lambda i: (i, 0)),
        ],
        out_specs=[
            pl.BlockSpec((TILE, rows), lambda i: (i, 0)),
            pl.BlockSpec((1, 1, rows), lambda i: (i, 0, 0)),
            pl.BlockSpec((2, rows), lambda i: (0, 0)),
        ],
        out_shape=[
            jax.ShapeDtypeStruct((count, rows), f32),
            jax.ShapeDtypeStruct((tiles, 1, rows), f32),
            jax.ShapeDtypeStruct((2, rows), f32),
        ],
        scratch_shapes=[pltpu.VMEM((rows, width), bf16), pltpu.VMEM((8, rows), f32)],
        compiler_params=pltpu.CompilerParams(vmem_limit_bytes=VMEM_BYTES),
        cost_estimate=pl.CostEstimate(
            flops=2 * rows * width * count, bytes_accessed=count * (4 * rows + 2 * width), transcendentals=rows * count
        ),
        name="row_stats",
    )(rot, centroids)


def cross_kernel(tiles, exp_ref, tile_top_ref, stat_ref, cent_ref, emb_ref, cross_ref, acc):
    step = pl.program_id(0)
    factor = jnp.exp(tile_top_ref[0] - stat_ref[0:1, :]) * stat_ref[1:2, :]
    weights = (exp_ref[...] * factor).astype(bf16)
    part = dot(weights, cent_ref[...], 0, 0)

    @pl.when(step == 0)
    def _():
        acc[...] = part

    @pl.when(step > 0)
    def _():
        acc[...] += part

    @pl.when(step == tiles - 1)
    def _():
        rebuilt = acc[...]
        high = rebuilt.astype(bf16)
        low = (rebuilt - high.astype(f32)).astype(bf16)
        emb = emb_ref[...]
        cross_ref[...] = dot(emb, high, 0, 0) + dot(emb, low, 0, 0)


def cross_partial(exps, tile_tops, stats, centroids, embeddings):
    count, rows = exps.shape
    width = centroids.shape[1]
    tiles = count // TILE
    return pl.pallas_call(
        functools.partial(cross_kernel, tiles),
        grid=(tiles,),
        in_specs=[
            pl.BlockSpec((TILE, rows), lambda i: (i, 0)),
            pl.BlockSpec((1, 1, rows), lambda i: (i, 0, 0)),
            pl.BlockSpec((2, rows), lambda i: (0, 0)),
            pl.BlockSpec((TILE, width), lambda i: (i, 0)),
            pl.BlockSpec((rows, width), lambda i: (0, 0)),
        ],
        out_specs=pl.BlockSpec((width, width), lambda i: (0, 0)),
        out_shape=jax.ShapeDtypeStruct((width, width), f32),
        scratch_shapes=[pltpu.VMEM((rows, width), f32)],
        compiler_params=pltpu.CompilerParams(vmem_limit_bytes=VMEM_BYTES),
        cost_estimate=pl.CostEstimate(
            flops=2 * rows * width * count, bytes_accessed=count * (4 * rows + 2 * width), transcendentals=0
        ),
        name="cross_partial",
    )(exps, tile_tops, stats, centroids, embeddings)


def sums_kernel(scale, rows_ref, stat_ref, cent_ref, sums_ref, counts_ref, rows_s):
    @pl.when(pl.program_id(0) == 0)
    def _():
        rows_s[...] = rows_ref[...].astype(bf16)

    cents = cent_ref[0].astype(bf16)
    rot = rows_s[...]
    scores = (dot(cents, rot, 1, 1) - half_norms(cents)) * scale
    weights = (jnp.exp(scores - stat_ref[0:1, :]) * stat_ref[1:2, :]).astype(bf16)
    sums_ref[0] = dot(weights, rot, 1, 0)
    counts = jnp.sum(weights.astype(f32), axis=1, keepdims=True)
    counts_ref[0] = jnp.broadcast_to(counts, counts_ref.shape[1:])


def cent_partial(rows, stats, blocks, scale):
    count, width = rows.shape
    number, block, _ = blocks.shape
    return pl.pallas_call(
        functools.partial(sums_kernel, scale),
        grid=(number,),
        in_specs=[
            pl.BlockSpec((count, width), lambda i: (0, 0)),
            pl.BlockSpec((2, count), lambda i: (0, 0)),
            pl.BlockSpec((1, block, width), lambda i: (i, 0, 0)),
        ],
        out_specs=[
            pl.BlockSpec((1, block, width), lambda i: (i, 0, 0)),
            pl.BlockSpec((1, block, 128), lambda i: (i, 0, 0)),
        ],
        out_shape=[
            jax.ShapeDtypeStruct((number, block, width), f32),
            jax.ShapeDtypeStruct((number, block, 128), f32),
        ],
        scratch_shapes=[pltpu.VMEM((count, width), bf16)],
        compiler_params=pltpu.CompilerParams(vmem_limit_bytes=VMEM_BYTES),
        cost_estimate=pl.CostEstimate(
            flops=4 * count * width * number * block,
            bytes_accessed=8 * number * block * width + 4 * count * width,
            transcendentals=count * number * block,
        ),
        name="cent_partial",
    )(rows, stats, blocks)


def polar_kernel(cross_ref, out_ref, half_s):
    cross = cross_ref[...]
    unit = cross * lax.rsqrt(jnp.sum(cross * cross, keepdims=True) + EPSILON)
    half = unit.astype(bf16)
    half_s[...] = half
    gram_once = dot(half, half, 0, 0)
    gram_half = gram_once.astype(bf16)
    gram_twice = dot(gram_half, gram_half, 1, 0)
    norm_power = jnp.sum(gram_twice * gram_twice, keepdims=True) + EPSILON
    inverse = 1.0 / jnp.sqrt(jnp.sqrt(jnp.sqrt(norm_power)))
    product = dot(half_s[...], gram_half, 1, 0) * (inverse * inverse)
    out_ref[...] = (1.5 * unit - 0.5 * product) * inverse

    @pl.loop(1, NS_ITERS)
    def _(_):
        half_s[...] = out_ref[...].astype(bf16)
        inner = dot(half_s[...], half_s[...], 0, 0).astype(bf16)
        out_ref[...] = 1.5 * out_ref[...] - 0.5 * dot(half_s[...], inner, 1, 0)


def polar_update(cross):
    width = cross.shape[0]
    return pl.pallas_call(
        polar_kernel,
        in_specs=[pl.BlockSpec(memory_space=pltpu.VMEM)],
        out_specs=pl.BlockSpec(memory_space=pltpu.VMEM),
        out_shape=jax.ShapeDtypeStruct((width, width), f32),
        scratch_shapes=[
            pltpu.VMEM((width, width), bf16),
        ],
        compiler_params=pltpu.CompilerParams(vmem_limit_bytes=VMEM_BYTES),
        cost_estimate=pl.CostEstimate(flops=18 * width**3, bytes_accessed=8 * width**2, transcendentals=0),
        name="polar_update",
    )(cross)


def solution(mesh):
    dp, cent = mesh.shape["dp"], mesh.shape["cent"]
    sizes = {"dp": dp, "cent": cent}
    cent_bits = [1 << k for k in range(cent.bit_length() - 1)]
    dp_bits = [1 << k for k in range(dp.bit_length() - 1)]

    def swap(value, axis, bit):
        return lax.ppermute(value, axis, [(i, i ^ bit) for i in range(sizes[axis])])

    def is_upper(axis, bit):
        return lax.rem(lax.div(lax.axis_index(axis), bit), 2)

    def halve(value, axis, bit):
        side, half = is_upper(axis, bit), value.shape[0] // 2
        sent = lax.dynamic_slice_in_dim(value, (1 - side) * half, half, 0)
        kept = lax.dynamic_slice_in_dim(value, side * half, half, 0)
        return kept + swap(sent, axis, bit)

    def double(value, axis, bit):
        other = swap(value, axis, bit)
        upper = is_upper(axis, bit) == 1
        return jnp.concatenate([jnp.where(upper, other, value), jnp.where(upper, value, other)])

    def after(value, earlier):
        return lax.optimization_barrier((value, earlier))[0]

    def sum_part(value, halved, added, earlier):
        for axis, bit in halved:
            value = halve(value, axis, bit)
        for axis, bit in added:
            value = value + swap(value, axis, bit)
        value = after(value, earlier)
        for axis, bit in reversed(halved):
            value = double(value, axis, bit)
        return value

    def sum_everywhere(value, earlier):
        value = halve(value, "cent", 1)
        rows = value.shape[0] // 2
        rest = [("dp", bit) for bit in dp_bits[1:]] + [("cent", bit) for bit in cent_bits[2:]]
        first = sum_part(value[:rows], [("cent", 2), ("dp", 1)], rest, earlier)
        second = sum_part(value[rows:], [("dp", 1), ("cent", 2)], rest, earlier)
        return double(jnp.concatenate([first, second]), "cent", 1)

    def body(embeddings, centroids, rotation):
        rows, width = embeddings.shape
        scale = SHARPNESS / math.sqrt(width)
        share = rows // GROUP
        block = centroids.shape[0] // dp
        dp_index = lax.axis_index("dp")
        cent_index = lax.axis_index("cent")
        first_row = lax.rem(cent_index, GROUP) * share

        rotated = jnp.dot(embeddings.astype(f32), rotation, precision=lax.Precision.HIGHEST)
        rotated = lax.reduce_precision(rotated, 8, 7)

        own_rows = lax.dynamic_slice_in_dim(rotated, first_row, share, 0)
        own_rows = lax.optimization_barrier(own_rows)
        all_rows = lax.all_gather(own_rows, "dp", axis=0, tiled=True)

        own_block = lax.dynamic_slice_in_dim(centroids, dp_index * block, block, 0)
        own_block = lax.optimization_barrier(own_block.astype(f32))
        x_block = swap(own_block, "cent", 2)

        exps, tile_tops, local = row_stats(after(rotated, own_rows), centroids, scale)
        top, total = local[:1], local[1:]
        for bit in cent_bits:
            other = swap(jnp.concatenate([top, total]), "cent", bit)
            new_top = jnp.maximum(top, other[:1])
            total = total * jnp.exp(top - new_top) + other[1:] * jnp.exp(other[:1] - new_top)
            top = new_top
        stats = jnp.concatenate([top, 1.0 / total])

        partial = cross_partial(exps, tile_tops, stats, centroids, embeddings)
        cross = sum_everywhere(partial, all_rows)

        pair = jnp.stack([own_block, after(x_block, partial)])
        other_pair = swap(pair, "cent", 1)
        blocks = jnp.concatenate([pair, other_pair])
        all_stats = after(lax.dynamic_slice_in_dim(stats, first_row, share, 1), partial)[None]
        for bit in dp_bits:
            all_stats = double(all_stats, "dp", bit)
        all_stats = jnp.swapaxes(all_stats, 0, 1).reshape(2, dp * share)
        sums, counts = cent_partial(all_rows, after(all_stats, cross), blocks, scale)
        new_rotation = polar_update(after(cross, counts))
        sums = sums[:2] + swap(sums[2:], "cent", 1)
        counts = counts[..., 0]
        counts = counts[:2] + swap(counts[2:], "cent", 1)
        sums = sums[0] + swap(sums[1], "cent", 2)
        counts = counts[0] + swap(counts[1], "cent", 2)
        new_centroids = (sums + PRIOR_WEIGHT * own_block) / (counts + PRIOR_WEIGHT)[:, None]
        return new_centroids, new_rotation

    in_specs = (P("dp", None), P("cent", None), P())
    out_specs = (P(("cent", "dp"), None), P())
    return jax.shard_map(body, mesh=mesh, in_specs=in_specs, out_specs=out_specs, check_vma=False)
```
